32 devices in a mesh: shard: 16 (over z, y, x), rep: 2 (over core).
Axes of the slice: x: 2, y: 2, z: 4, core: 2. Of those that a mesh axis runs over, the one named last changes fastest.
Arguments:
- tokens: bfloat16 [16384, 576], P(('shard', 'rep')), may hold values from -30 to 30
- cotangent: bfloat16 [16384, 576], P(('shard', 'rep')), may hold values from -6 to 6
- attention_gain: bfloat16 [576], P('shard'), may hold values from 0.5 to 1.5
- query_weight: bfloat16 [576, 576], P('shard'), may hold values from -0.2482166 to 0.2482166
- key_weight: bfloat16 [576, 192], P('shard'), may hold values from -0.2482166 to 0.2482166
- value_weight: bfloat16 [576, 192], P('shard'), may hold values from -0.25 to 0.25
- output_weight: bfloat16 [576, 576], P('shard'), may hold values from -1 to 1
- feedforward_gain: bfloat16 [576], P('shard'), may hold values from 0.5 to 1.5
- gate_weight: bfloat16 [576, 1536], P('shard'), may hold values from -0.25 to 0.25
- up_weight: bfloat16 [576, 1536], P('shard'), may hold values from -0.25 to 0.25
- down_weight: bfloat16 [1536, 576], P('shard'), may hold values from -0.15625 to 0.15625
Outputs:
- layer_output: bfloat16 [16384, 576], P(('shard', 'rep'))
- grad_tokens: bfloat16 [16384, 576], P(('shard', 'rep'))
- grad_attention_gain: float32 [576], P('shard')
- grad_query: float32 [576, 576], P('shard')
- grad_key: float32 [576, 192], P('shard')
- grad_value: float32 [576, 192], P('shard')
- grad_output: float32 [576, 576], P('shard')
- grad_feedforward_gain: float32 [576], P('shard')
- grad_gate: float32 [576, 1536], P('shard')
- grad_up: float32 [576, 1536], P('shard')
- grad_down: float32 [1536, 576], P('shard')
The draws below stay inside these ranges and needn't reach their ends.
All inputs are finite; a program needn't handle non-finite values.
Results may differ from the reference program's by a relative error of at most 0.014.
The reference program's roundings to bfloat16 on the way count: a program that leaves them out, or rounds other values in their place, can miss the bound.
Values may be sent and summed in bfloat16 or wider, within the bound.
No kernel may reach another device: no remote copies, remote signals or barrier semaphores. Data moves between devices by JAX's collectives and lax.ppermute only.
A program may use at most 128 MiB of HBM per device.

```python
import math
import jax
import jax.numpy as jnp
from jax import lax

D = 576
H = 9
KV = 3
HD = 64
FF = 1536
TOK_DEV = 512
TOKENS = 16384
N_SHARD = 16


def draw_tokens(key, part):
    noise_part = jax.random.truncated_normal(jax.random.fold_in(key, 7101), -6.0, 6.0, (TOKENS, D), jnp.float32)
    blocks = TOKENS // TOK_DEV
    pairing = jax.random.permutation(jax.random.fold_in(key, 7102), blocks) % N_SHARD
    row_block = jnp.arange(TOKENS) // TOK_DEV
    col_block = jnp.arange(D) // (D // N_SHARD)
    paired_block = pairing[row_block]
    noise_part = noise_part * jnp.where(paired_block[:, None] == col_block[None, :], 3.0, 1.0)
    return noise_part.astype(jnp.bfloat16)


def draw_query_weight(key, part):
    matrix = jax.random.truncated_normal(jax.random.fold_in(key, 7201), -4.0, 4.0, (D, D), jnp.float32) / D ** 0.5
    return matrix.astype(jnp.bfloat16)


def draw_key_weight(key, part):
    matrix = jax.random.truncated_normal(jax.random.fold_in(key, 7301), -4.0, 4.0, (D, KV * HD), jnp.float32) / D ** 0.5
    return matrix.astype(jnp.bfloat16)


def steps_of(own_key, dims, shards, least, high):
    factor_of = 1.0
    for dim, parts in shards:
        heights = jax.random.uniform(jax.random.fold_in(jax.random.fold_in(own_key, 6), dim), (parts,), jnp.float32, least / len(shards), high / len(shards))
        factor_of = factor_of * jnp.repeat(jnp.exp(heights), dims[dim] // parts).reshape((-1,) + (1,) * (len(dims) - 1 - dim))
    return factor_of


def noise(key, shape, scale, bound, cuts=(), kind=jnp.bfloat16):
    values = scale * jax.random.normal(key, shape, jnp.float32)
    if cuts:
        values = values * steps_of(key, shape, cuts, -0.22, 0.18)
    return jnp.clip(values, -bound, bound).astype(kind)


def setup_inputs(seed: int = 0) -> dict:
    splits = jax.random.split(jax.random.key(seed), 12)
    tokens = draw_tokens(jax.random.fold_in(splits[11], 71), 0)
    cotangent = noise(splits[1], (TOKENS, D), 1.0, 6.0, ((0, 32),))
    attention_gain = jnp.clip(1.0 + 0.1 * jax.random.normal(splits[2], (D,), jnp.float32), 0.5, 1.5).astype(jnp.bfloat16)
    query_weight = draw_query_weight(jax.random.fold_in(splits[11], 71), 0)
    key_weight = draw_key_weight(jax.random.fold_in(splits[11], 71), 0)
    value_weight = noise(splits[5], (D, KV * HD), D ** -0.5, 0.25, ((0, 16),))
    output_weight = noise(splits[6], (D, D), (D // 16) ** -0.5, 1.0, ((0, 16),))
    feedforward_gain = jnp.clip(1.0 + 0.1 * jax.random.normal(splits[7], (D,), jnp.float32), 0.5, 1.5).astype(jnp.bfloat16)
    gate_weight = noise(splits[8], (D, FF), D ** -0.5, 0.25, ((0, 16),))
    up_weight = noise(splits[9], (D, FF), D ** -0.5, 0.25, ((0, 16),))
    down_weight = noise(splits[10], (FF, D), FF ** -0.5, 0.15625, ((0, 16),))
    return dict(tokens=tokens, cotangent=cotangent, attention_gain=attention_gain, query_weight=query_weight, key_weight=key_weight, value_weight=value_weight, output_weight=output_weight, feedforward_gain=feedforward_gain, gate_weight=gate_weight, up_weight=up_weight, down_weight=down_weight)


EPSILON = 1e-05
HIGHEST = lax.Precision.HIGHEST

@jax.custom_vjp
def low(v):
    return lax.optimization_barrier(v.astype(jnp.bfloat16)).astype(jnp.float32)

@jax.custom_vjp
def low_back(v):
    return v

def low_keep(v):
    return (low(v), None)

def low_pass(kept, grad):
    return (grad,)

def back_keep(v):
    return (v, None)

def back_low(kept, grad):
    return (low(grad),)
low.defvjp(low_keep, low_pass)
low_back.defvjp(back_keep, back_low)

def matmul_high(former, latter):
    return jnp.dot(former, latter, precision=HIGHEST)

def rope_tables(length):
    half_size = HD // 2
    frequency = 10000.0 ** (-2.0 * jnp.arange(half_size, dtype=jnp.float32) / HD)
    angles = jnp.arange(length, dtype=jnp.float32)[:, None] * frequency[None, :]
    angles = jnp.concatenate([angles, angles], axis=1)
    return (jnp.cos(angles)[:, None, :], jnp.sin(angles)[:, None, :])

def rotate(values):
    half_size = values.shape[-1] // 2
    return jnp.concatenate([-values[..., half_size:], values[..., :half_size]], axis=-1)

def rms_scale(values):
    return lax.rsqrt(lax.optimization_barrier(jnp.mean(values * values, axis=-1, keepdims=True)) + EPSILON)

def decoder_layer(inputs, gain_one, query_mat, key_mat, value_mat, out_mat, gain_two, gate_mat, up_mat, down_mat):
    length = inputs.shape[0]
    group_size = H // KV
    scale_factor = HD ** (-0.5)
    cos_table, sin_table = rope_tables(length)
    normed_one = low(inputs * rms_scale(inputs) * gain_one)
    queries = low_back(matmul_high(normed_one, query_mat)).reshape(length, H, HD)
    key_proj = low_back(matmul_high(normed_one, key_mat)).reshape(length, KV, HD)
    values = low(low_back(matmul_high(normed_one, value_mat))).reshape(length, KV, HD)
    query_rot = low(queries * cos_table + rotate(queries) * sin_table).reshape(length, KV, group_size, HD)
    key_rot = low(key_proj * cos_table + rotate(key_proj) * sin_table)
    causal = lax.broadcasted_iota(jnp.int32, (length, length), 0) >= lax.broadcasted_iota(jnp.int32, (length, length), 1)
    raw_scores = jnp.einsum('qgjd,kgd->gjqk', query_rot, key_rot, precision=HIGHEST)
    scores = low_back(jnp.where(causal, raw_scores * scale_factor, -1e+30))
    row_top = lax.optimization_barrier(jnp.max(scores, axis=-1, keepdims=True))
    log_total = row_top + jnp.log(lax.optimization_barrier(jnp.sum(jnp.exp(scores - row_top), axis=-1, keepdims=True)))
    probability = low(jnp.exp(scores - log_total))
    context = jnp.einsum('gjqk,kgd->qgjd', probability, values, precision=HIGHEST).reshape(length, H * HD)
    context = low(low_back(context))
    hidden = inputs + low_back(matmul_high(context, out_mat))
    normed_two = low(hidden * rms_scale(hidden) * gain_two)
    gate_pre = low_back(matmul_high(normed_two, gate_mat))
    up_proj = low_back(matmul_high(normed_two, up_mat))
    active = low(jax.nn.silu(gate_pre) * up_proj)
    return hidden + low_back(matmul_high(active, down_mat))

def reference(tokens, cotangent, attention_gain, query_weight, key_weight, value_weight, output_weight, feedforward_gain, gate_weight, up_weight, down_weight):
    weights = tuple((item.astype(jnp.float32) for item in (attention_gain, query_weight, key_weight, value_weight, output_weight, feedforward_gain, gate_weight, up_weight, down_weight)))
    sequences = TOKENS // TOK_DEV
    group_count = math.gcd(sequences, max(1, 4096 // TOK_DEV))
    token_groups = tokens.astype(jnp.float32).reshape(sequences // group_count, group_count, TOK_DEV, D)
    cot_groups = cotangent.astype(jnp.float32).reshape(sequences // group_count, group_count, TOK_DEV, D)

    def forward_group(inputs, *params):
        return jax.vmap(lambda single: decoder_layer(single, *params))(inputs)

    def group_step(summed, group_item):
        inputs, cot_item = group_item
        outputs, pullback = jax.vjp(forward_group, inputs, *weights)
        gradients = pullback(cot_item)
        summed = tuple((prior + fresh for prior, fresh in zip(summed, gradients[1:])))
        return (summed, (outputs.astype(jnp.bfloat16), gradients[0].astype(jnp.bfloat16)))
    zero_sums = tuple((jnp.zeros_like(item) for item in weights))
    summed, (outputs, grad_inputs) = lax.scan(group_step, zero_sums, (token_groups, cot_groups))
    return (outputs.reshape(TOKENS, D), grad_inputs.reshape(TOKENS, D), summed[0], summed[1], summed[2], summed[3], summed[4], summed[5], summed[6], summed[7], summed[8])
```

```python
import jax
import jax.numpy as jnp
from jax import lax
from jax.sharding import PartitionSpec as P

H = 9
KV = 3
HD = 64


EPSILON = 1e-05


def contract_rows(former, latter):
    return lax.dot_general(
        former, latter, (((0,), (0,)), ((), ())), preferred_element_type=jnp.float32
    )


def contract_cols(former, latter):
    return lax.dot_general(
        former, latter, (((1,), (1,)), ((), ())), preferred_element_type=jnp.float32
    )


def rope_tables(length):
    half_size = HD // 2
    frequency = 10000.0 ** (-2.0 * jnp.arange(half_size, dtype=jnp.float32) / HD)
    angles = jnp.arange(length, dtype=jnp.float32)[:, None] * frequency[None, :]
    angles = jnp.concatenate([angles, angles], axis=1)
    return (jnp.cos(angles)[:, None, :], jnp.sin(angles)[:, None, :])


def rotate(values):
    half_size = values.shape[-1] // 2
    return jnp.concatenate([-values[..., half_size:], values[..., :half_size]], axis=-1)


def norm_forward(values, gain):
    scale_rows = lax.rsqrt(jnp.mean(values * values, axis=-1, keepdims=True) + EPSILON)
    normed = values * scale_rows
    return (normed, scale_rows, (normed * gain).astype(jnp.bfloat16))


def norm_backward(grad_normed_gain, normed, scale_rows, gain):
    grad_gain = jnp.sum(grad_normed_gain * normed, axis=0)
    grad_normed = grad_normed_gain * gain
    grad_input = scale_rows * (
        grad_normed - normed * jnp.mean(grad_normed * normed, axis=-1, keepdims=True)
    )
    return (grad_input, grad_gain)


def attention_scores(query_rot, key_rot, causal, scale_factor):
    raw_scores = jnp.einsum(
        "qgjd,kgd->gjqk", query_rot, key_rot, preferred_element_type=jnp.float32
    )
    return jnp.where(causal, raw_scores * scale_factor, -1e30)


def phases_of(n):
    out, stride = [], 1
    while stride < n:
        size = 4 if n // stride % 4 == 0 else 2
        out.append((stride, size))
        stride *= size
    return out


def groups_of(n, stride, size):
    return [
        [base + stride * j for j in range(size)]
        for base in range(n)
        if base // stride % size == 0
    ]


def swap_cores(value):
    return lax.ppermute(value, "rep", [(0, 1), (1, 0)])


def gather_half(n, block):
    rows, cols = block.shape
    held = block[None]
    dims = []
    for stride, size in reversed(phases_of(n)):
        sent = jnp.broadcast_to(held[None], (size,) + held.shape)
        held = lax.all_to_all(
            sent, "shard", 0, 0, tiled=True, axis_index_groups=groups_of(n, stride, size)
        )
        held = held.reshape((-1, rows, cols))
        dims.append(size)
    held = held.reshape(tuple(reversed(dims)) + (rows, cols))
    order = tuple(reversed(range(len(dims)))) + (len(dims), len(dims) + 1)
    return held.transpose(order).reshape((n, rows, cols))


def gather_pair(n, first, second):
    core = lax.axis_index("rep")
    mine = gather_half(n, jnp.where(core == 0, first, second))
    other = swap_cores(mine)
    return jnp.where(core == 0, mine, other), jnp.where(core == 0, other, mine)


def scatter_pair(n, first, second):
    core = lax.axis_index("rep")
    first, second = first.astype(jnp.bfloat16), second.astype(jnp.bfloat16)
    keep = jnp.where(core == 0, first, second)
    send = jnp.where(core == 0, second, first)
    held = keep.astype(jnp.float32) + swap_cores(send).astype(jnp.float32)
    rows, cols = held.shape[1:]
    sizes = [size for _, size in phases_of(n)]
    for stride, size in phases_of(n):
        held = held.astype(jnp.bfloat16)
        left = held.shape[0] // size
        sent = held.reshape((left, size, rows, cols)).swapaxes(0, 1)
        got = lax.all_to_all(
            sent, "shard", 0, 0, tiled=True, axis_index_groups=groups_of(n, stride, size)
        )
        held = jnp.sum(got.astype(jnp.float32), axis=0)
    mine = held[0]
    other = swap_cores(mine)
    return jnp.where(core == 0, mine, other), jnp.where(core == 0, other, mine)


def per_device(
    n,
    tokens,
    cotangent,
    attention_gain,
    query_weight,
    key_weight,
    value_weight,
    output_weight,
    feedforward_gain,
    gate_weight,
    up_weight,
    down_weight,
):
    length, width = tokens.shape
    group_size = H // KV
    scale_factor = HD ** (-0.5)
    own_rows = width // n
    q_cols, kv_cols = H * HD, KV * HD
    cos_table, sin_table = rope_tables(length)
    causal = lax.broadcasted_iota(jnp.int32, (length, length), 0) >= lax.broadcasted_iota(
        jnp.int32, (length, length), 1
    )

    def with_gain(weights, gain):
        row = jnp.pad(gain, (0, weights.shape[1] - gain.shape[0]))
        return jnp.concatenate([weights, row[None]], axis=0)

    first, second = gather_pair(
        n,
        with_gain(jnp.concatenate([query_weight, key_weight], axis=1), attention_gain),
        with_gain(jnp.concatenate([value_weight, output_weight], axis=1), feedforward_gain),
    )
    query_mat = first[:, :own_rows, :q_cols].reshape((width, q_cols))
    key_mat = first[:, :own_rows, q_cols:].reshape((width, kv_cols))
    value_mat = second[:, :own_rows, :kv_cols].reshape((width, kv_cols))
    out_mat = second[:, :own_rows, kv_cols:].reshape((q_cols, width))
    gain_one = first[:, own_rows, :own_rows].reshape((width,)).astype(jnp.float32)
    gain_two = second[:, own_rows, :own_rows].reshape((width,)).astype(jnp.float32)

    gate_mat, up_mat = gather_pair(n, gate_weight, up_weight)
    gate_mat = gate_mat.reshape((width, -1))
    up_mat = up_mat.reshape((width, -1))
    down_rows = down_weight.shape[0]
    down_first, down_second = gather_pair(
        n, down_weight[: down_rows // 2], down_weight[down_rows // 2 :]
    )
    down_mat = jnp.concatenate([down_first, down_second], axis=1).reshape((-1, width))

    inputs = tokens.astype(jnp.float32)
    normed_one, scale_one, normed_low = norm_forward(inputs, gain_one)
    queries = jnp.dot(normed_low, query_mat, preferred_element_type=jnp.float32).reshape(
        length, H, HD
    )
    key_proj = jnp.dot(normed_low, key_mat, preferred_element_type=jnp.float32).reshape(
        length, KV, HD
    )
    values_low = (
        jnp.dot(normed_low, value_mat, preferred_element_type=jnp.float32)
        .astype(jnp.bfloat16)
        .reshape(length, KV, HD)
    )
    query_rot = (
        (queries * cos_table + rotate(queries) * sin_table)
        .astype(jnp.bfloat16)
        .reshape(length, KV, group_size, HD)
    )
    key_rot = (key_proj * cos_table + rotate(key_proj) * sin_table).astype(jnp.bfloat16)
    scores = attention_scores(query_rot, key_rot, causal, scale_factor)
    row_top = jnp.max(scores, axis=-1, keepdims=True)
    log_total = row_top + jnp.log(jnp.sum(jnp.exp(scores - row_top), axis=-1, keepdims=True))
    probs_low = jnp.exp(scores - log_total).astype(jnp.bfloat16)
    context_low = (
        jnp.einsum("gjqk,kgd->qgjd", probs_low, values_low, preferred_element_type=jnp.float32)
        .reshape(length, H * HD)
        .astype(jnp.bfloat16)
    )
    hidden = inputs + jnp.dot(context_low, out_mat, preferred_element_type=jnp.float32)
    normed_two, scale_two, hidden_low = norm_forward(hidden, gain_two)
    gate_pre = jnp.dot(hidden_low, gate_mat, preferred_element_type=jnp.float32)
    up_proj = jnp.dot(hidden_low, up_mat, preferred_element_type=jnp.float32)
    active_low = (jax.nn.silu(gate_pre) * up_proj).astype(jnp.bfloat16)
    layer_output = (
        hidden + jnp.dot(active_low, down_mat, preferred_element_type=jnp.float32)
    ).astype(jnp.bfloat16)
    grad_out = cotangent.astype(jnp.float32)
    grad_down = contract_rows(active_low, cotangent).reshape((n, 2, down_rows // 2, width))
    owned_down = jnp.concatenate(scatter_pair(n, grad_down[:, 0], grad_down[:, 1]), axis=0)
    grad_active = contract_cols(cotangent, down_mat)
    sigmoid_gate = jax.nn.sigmoid(gate_pre)
    grad_up_low = (grad_active * gate_pre * sigmoid_gate).astype(jnp.bfloat16)
    grad_gate_low = (
        grad_active * up_proj * sigmoid_gate * (1.0 + gate_pre * (1.0 - sigmoid_gate))
    ).astype(jnp.bfloat16)
    grad_gate = contract_rows(hidden_low, grad_gate_low)
    grad_up = contract_rows(hidden_low, grad_up_low)
    owned_gate, owned_up = scatter_pair(
        n, grad_gate.reshape((n, own_rows, -1)), grad_up.reshape((n, own_rows, -1))
    )
    grad_hidden_low = contract_cols(grad_gate_low, gate_mat) + contract_cols(grad_up_low, up_mat)
    grad_from_two, grad_gain_two = norm_backward(grad_hidden_low, normed_two, scale_two, gain_two)
    grad_hidden = grad_out + grad_from_two
    grad_attn_low = grad_hidden.astype(jnp.bfloat16)
    grad_output = contract_rows(context_low, grad_attn_low)
    grad_context_low = (
        contract_cols(grad_attn_low, out_mat)
        .astype(jnp.bfloat16)
        .reshape(length, KV, group_size, HD)
    )
    scores_again = attention_scores(query_rot, key_rot, causal, scale_factor)
    probability = jnp.exp(scores_again - log_total)
    probs_again = probability.astype(jnp.bfloat16)
    grad_probs = jnp.einsum(
        "qgjd,kgd->gjqk", grad_context_low, values_low, preferred_element_type=jnp.float32
    )
    grad_values_low = (
        jnp.einsum(
            "gjqk,qgjd->kgd", probs_again, grad_context_low, preferred_element_type=jnp.float32
        )
        .astype(jnp.bfloat16)
        .reshape(length, KV * HD)
    )
    grad_scores = probability * (
        grad_probs - jnp.sum(probability * grad_probs, axis=-1, keepdims=True)
    )
    grad_scores_low = grad_scores.astype(jnp.bfloat16)
    grad_query_rot = (
        jnp.einsum("gjqk,kgd->qgjd", grad_scores_low, key_rot, preferred_element_type=jnp.float32)
        * scale_factor
    ).reshape(length, H, HD)
    grad_key_rot = (
        jnp.einsum("gjqk,qgjd->kgd", grad_scores_low, query_rot, preferred_element_type=jnp.float32)
        * scale_factor
    )
    grad_query_low = (
        (grad_query_rot * cos_table - rotate(grad_query_rot * sin_table))
        .astype(jnp.bfloat16)
        .reshape(length, H * HD)
    )
    grad_key_low = (
        (grad_key_rot * cos_table - rotate(grad_key_rot * sin_table))
        .astype(jnp.bfloat16)
        .reshape(length, KV * HD)
    )
    grad_query = contract_rows(normed_low, grad_query_low)
    grad_key = contract_rows(normed_low, grad_key_low)
    grad_value = contract_rows(normed_low, grad_values_low)
    grad_normed_low = (
        contract_cols(grad_query_low, query_mat)
        + contract_cols(grad_key_low, key_mat)
        + contract_cols(grad_values_low, value_mat)
    )
    grad_from_one, grad_gain_one = norm_backward(grad_normed_low, normed_one, scale_one, gain_one)
    grad_tokens = (grad_hidden + grad_from_one).astype(jnp.bfloat16)

    def grads_with_gain(left, right, gain):
        both = jnp.concatenate([left, right], axis=1)
        row = jnp.pad(gain.reshape((n, 1, own_rows)), ((0, 0), (0, 0), (0, both.shape[1] - own_rows)))
        return jnp.concatenate([both.reshape((n, own_rows, -1)), row], axis=1)

    owned_first, owned_second = scatter_pair(
        n,
        grads_with_gain(grad_query, grad_key, grad_gain_one),
        grads_with_gain(grad_value, grad_output, grad_gain_two),
    )
    return (
        layer_output,
        grad_tokens,
        owned_first[own_rows, :own_rows],
        owned_first[:own_rows, :q_cols],
        owned_first[:own_rows, q_cols:],
        owned_second[:own_rows, :kv_cols],
        owned_second[:own_rows, kv_cols:],
        owned_second[own_rows, :own_rows],
        owned_gate,
        owned_up,
        owned_down,
    )


def solution(mesh):
    n = mesh.shape["shard"]
    tokens = P(("shard", "rep"), None)
    matrix = P("shard", None)
    vector = P("shard")

    def layer(*args):
        return per_device(n, *args)

    return jax.shard_map(
        layer,
        mesh=mesh,
        in_specs=(tokens, tokens, vector, matrix, matrix, matrix, matrix, vector)
        + (matrix,) * 3,
        out_specs=(tokens, tokens, vector, matrix, matrix, matrix, matrix, vector)
        + (matrix,) * 3,
        check_vma=False,
    )
```
